256 devices in a mesh: azim: 32 (over z, x_lo, core), span: 8 (over x_hi, y).
Axes of the slice: x: 4 (x_hi: 2, x_lo: 2; x = x_hi * 2 + x_lo), y: 4, z: 8, core: 2. Of those that a mesh axis runs over, the one named last changes fastest.
Arguments:
- velocity: float32 [3, 3, 256, 32, 4, 512], P(None, None, 'azim', 'span'), may hold values from -1.8 to 1.8
- metric: float32 [3, 256, 32, 4, 512], P(None, 'azim', 'span'), may hold values from 0.5 to 2
- mortar_tables: float32 [8, 64, 64], replicated, may hold values from -0.75 to 0.75
- angle_step: int32 [1], replicated, may hold values from 0 to 31
- tile_face: int32 [32, 8, 64], P('azim', 'span'), may hold values from 0 to 31
- tile_side: int32 [32, 8, 64], P('azim', 'span'), may hold values from -1 to 1
- tile_slot: int32 [32, 8, 64], P('azim', 'span'), may hold values from 0 to 31
- tile_offset: int32 [32, 8, 64], P('azim', 'span'), may hold values from 0 to 7
Outputs:
- assembled_rhs: float32 [3, 256, 32, 4, 512], P(None, 'azim', 'span')
- stator_trace: float32 [8192, 3, 64], P(('azim', 'span'))
The draws below stay inside these ranges and needn't reach their ends.
Inputs may be any that keep to these rules, and one draw needn't show every extreme that they name: `tile_side`: -1 marks an empty tile.
All inputs are finite; a program needn't handle non-finite values.
Results may differ from the reference program's by a relative error of at most 0.00007.
Values sent between devices are 32-bit elements; how exact they have to be, the bound alone decides.
No kernel may reach another device: no remote copies, remote signals or barrier semaphores. Data moves between devices by JAX's collectives and lax.ppermute only.
A program may use at most 128 MiB of HBM per device.

```python
import math
import jax
import jax.numpy as jnp
import numpy as np
from jax import lax

NP = 8
FACE = 64
NODES = 512
NOFF = 8
EA = 8
ES = 4
ER = 4
TL = 64
STAT_DEV = 32
NA = 256
NS = 32
STAT = 8192
N_AZIM = 32
N_SPAN = 8


def set_ends(values, own_key, smallest, largest):
    place = [jax.random.randint(jax.random.fold_in(own_key, axis), (), 0, length) for axis, length in enumerate(values.shape)]
    longest = values.shape.index(max(values.shape))
    neighbour = place[:longest] + [(place[longest] + 1) % values.shape[longest]] + place[longest + 1:]
    return values.at[tuple(place)].set(smallest).at[tuple(neighbour)].set(largest)


def shard_levels(stream_key, dims, split, smallest, high):
    factor_of = 1.0
    for dim, blocks in split:
        draws = jax.random.uniform(jax.random.fold_in(jax.random.fold_in(stream_key, 6), dim), (blocks,), jnp.float32, smallest / len(split), high / len(split))
        factor_of = factor_of * jnp.repeat(jnp.exp(draws), dims[dim] // blocks).reshape((-1,) + (1,) * (len(dims) - 1 - dim))
    return factor_of


def gaussian(stream_key, extent, deviation, most, cuts=(), held_as=jnp.bfloat16):
    factor_of = shard_levels(stream_key, extent, cuts, -0.22, 0.18) if cuts else 1.0
    drawn = jax.random.normal(stream_key, extent, jnp.float32) * deviation * factor_of
    return jnp.minimum(jnp.maximum(drawn, -most), most).astype(held_as)


def setup_inputs(seed: int = 0) -> dict:
    streams_of = jax.random.split(jax.random.key(seed), 9)
    velocity = gaussian(streams_of[0], (3, 3, NA, NS, ER, NODES), 0.3, 1.8, ((2, 32), (3, 8)), jnp.float32)
    metric = jnp.clip(jnp.exp(math.log(2.0) - 1.3862944 * jax.random.uniform(streams_of[1], (3, NA, NS, ER, NODES), jnp.float32) ** shard_levels(streams_of[1], (3, NA, NS, ER, NODES), ((1, 32), (2, 8)), -0.2, 0.2)), 0.5, 2.0)
    mortar_tables = gaussian(streams_of[2], (NOFF, FACE, FACE), FACE ** -0.5, 0.75, (), jnp.float32)
    angle_step = jax.random.randint(streams_of[3], (1,), 0, N_AZIM).astype(jnp.int32)
    tile_face = set_ends(jax.random.randint(streams_of[4], (N_AZIM, N_SPAN, TL), 0, EA * ES), jax.random.fold_in(streams_of[4], 1), 0, (EA * ES) - 1).astype(jnp.int32)
    tile_side = set_ends(jax.random.randint(streams_of[5], (N_AZIM, N_SPAN, TL), -1, 2), jax.random.fold_in(streams_of[5], 1), -1, 1).astype(jnp.int32)
    tile_slot = set_ends(jax.random.randint(streams_of[6], (N_AZIM, N_SPAN, TL), 0, STAT_DEV), jax.random.fold_in(streams_of[6], 1), 0, STAT_DEV - 1).astype(jnp.int32)
    tile_offset = set_ends(jax.random.randint(streams_of[7], (N_AZIM, N_SPAN, TL), 0, NOFF), jax.random.fold_in(streams_of[7], 1), 0, NOFF - 1).astype(jnp.int32)
    return dict(velocity=velocity, metric=metric, mortar_tables=mortar_tables, angle_step=angle_step, tile_face=tile_face, tile_side=tile_side, tile_slot=tile_slot, tile_offset=tile_offset)


STEP_DT = 0.05


def legendre_rows(points, degree):
    rows = [points * 0.0 + 1.0, points]
    for level in range(2, degree + 1):
        rows.append(((2 * level - 1) * points * rows[-1] - (level - 1) * rows[-2]) / level)
    return rows


def spectral_tables():
    degree = NP - 1
    points = -np.cos(np.pi * np.arange(NP) / degree)
    for newton_step in range(60):
        rows = legendre_rows(points, degree)
        points = points - (points * rows[degree] - rows[degree - 1]) / (NP * rows[degree])
    rows = legendre_rows(points, degree)
    weights = 2.0 / (degree * NP * rows[degree] ** 2)
    spacing = points[:, None] - points[None, :] + np.eye(NP)
    matrix = rows[degree][:, None] / rows[degree][None, :] / spacing
    corner = np.concatenate([[-degree * NP / 4.0], np.zeros(NP - 2), [degree * NP / 4.0]])
    matrix = matrix * (1.0 - np.eye(NP)) + np.eye(NP) * corner[None, :]
    unit = np.eye(NP)
    along_azim = np.kron(np.eye(NP * NP), matrix)
    along_span = np.kron(unit, np.kron(matrix, unit))
    along_radius = np.kron(matrix, np.eye(NP * NP))
    derive = np.concatenate([along_azim.T, along_span.T, along_radius.T], axis=1)
    volume = np.kron(np.kron(weights, weights), weights)
    grid = np.arange(NP ** 3).reshape(NP, NP, NP)
    layers = [grid[:, :, 0], grid[:, :, -1], grid[:, 0, :], grid[:, -1, :], grid[0], grid[-1]]
    face_index = [jnp.asarray(layer.ravel(), dtype=jnp.int32) for layer in layers]
    return jnp.asarray(derive, jnp.float32), jnp.asarray(volume, jnp.float32), face_index


def history_parts(velocity):
    extrapolated = 3.0 * velocity[0] - 3.0 * velocity[1] + velocity[2]
    history = (3.0 * velocity[0] - 1.5 * velocity[1] + velocity[2] / 3.0) / STEP_DT
    return extrapolated, history


def local_terms(extrapolated, history, metric, derive, volume):
    nodes = extrapolated.shape[-1]
    flat = extrapolated.reshape(-1, nodes)
    slopes = jnp.dot(flat, derive, precision=lax.Precision.HIGHEST)
    slopes = slopes.reshape(extrapolated.shape[:-1] + (3, nodes))
    advect = extrapolated * metric
    convection = advect[0] * slopes[..., 0, :] + advect[1] * slopes[..., 1, :]
    convection = convection + advect[2] * slopes[..., 2, :]
    mass = volume / (metric[0] * metric[1] * metric[2])
    return mass * (history - convection)


def join_faces(values, along, lower_nodes, upper_nodes, upstream, downstream):
    lower_face = jnp.take(values, lower_nodes, axis=-1)
    upper_face = jnp.take(values, upper_nodes, axis=-1)
    count = values.shape[along]
    from_below = jnp.concatenate([upstream, lax.slice_in_dim(upper_face, 0, count - 1, axis=along)], axis=along)
    from_above = jnp.concatenate([lax.slice_in_dim(lower_face, 1, count, axis=along), downstream], axis=along)
    values = values.at[..., lower_nodes].add(from_below)
    return values.at[..., upper_nodes].add(from_above)


def zero_edge(values, along, width):
    edge_shape = list(values.shape)
    edge_shape[along] = 1
    edge_shape[-1] = width
    return jnp.zeros(tuple(edge_shape), jnp.float32)


def reference(velocity, metric, mortar_tables, angle_step, tile_face, tile_side, tile_slot, tile_offset):
    derive, volume, face_index = spectral_tables()
    extrapolated, history = history_parts(velocity)
    element_terms = local_terms(extrapolated, history, metric, derive, volume)
    upstream = lax.slice_in_dim(jnp.take(element_terms, face_index[1], axis=-1), NA - 1, NA, axis=1)
    downstream = lax.slice_in_dim(jnp.take(element_terms, face_index[0], axis=-1), 0, 1, axis=1)
    joined = join_faces(element_terms, 1, face_index[0], face_index[1], upstream, downstream)
    blank = zero_edge(joined, 2, FACE)
    joined = join_faces(joined, 2, face_index[2], face_index[3], blank, blank)
    blank = zero_edge(joined, 3, FACE)
    assembled_rhs = join_faces(joined, 3, face_index[4], face_index[5], blank, blank)

    surface = extrapolated[:, :, :, ER - 1, NODES - FACE:]
    rotor_faces = surface.reshape(3, N_AZIM, EA, N_SPAN, ES, FACE).transpose(1, 3, 2, 4, 0, 5)
    rotor_faces = rotor_faces.reshape(N_AZIM, N_SPAN, EA * ES, 3, FACE)
    picked = jnp.take_along_axis(rotor_faces, tile_face[:, :, :, None, None], axis=2)
    chosen = mortar_tables[tile_offset]
    tile_values = jnp.einsum("astpq,astcq->astcp", chosen, picked, precision=lax.Precision.HIGHEST)
    active = (tile_side >= 0).astype(jnp.float32)
    tile_values = tile_values * active[..., None, None]
    sector = jnp.arange(N_AZIM).astype(jnp.int32)[:, None, None]
    slab = jnp.arange(N_SPAN).astype(jnp.int32)[None, :, None]
    reader = (sector + angle_step[0] + tile_side) % N_AZIM
    target = ((reader * N_SPAN + slab) * STAT_DEV + tile_slot).astype(jnp.int32)
    stator_trace = jnp.zeros((STAT, 3, FACE), jnp.float32)
    stator_trace = stator_trace.at[target.reshape(-1)].add(tile_values.reshape(-1, 3, FACE))
    return assembled_rhs, stator_trace
```

```python
import jax
import jax.numpy as jnp
import numpy as np
from jax import lax
from jax.experimental import pallas as pl
from jax.experimental.pallas import tpu as pltpu
from jax.sharding import PartitionSpec as P

NP = 8
STEP_DT = 0.05
EA, ES, ER = 8, 4, 4
BLOCK = ES * 16
ROWS = EA * BLOCK
LANES = 128
TL = 64
NOFF = 8
SLOTS = 32
CHUNKS = 2
WIDE = EA // CHUNKS
F32 = jnp.float32
BF16 = jnp.bfloat16
LIMIT = 32 * 2**20


def legendre_rows(points, degree):
    rows = [points * 0.0 + 1.0, points]
    for level in range(2, degree + 1):
        rows.append(((2 * level - 1) * points * rows[-1] - (level - 1) * rows[-2]) / level)
    return rows


def spectral_tables():
    degree = NP - 1
    points = -np.cos(np.pi * np.arange(NP) / degree)
    for newton_step in range(60):
        rows = legendre_rows(points, degree)
        points = points - (points * rows[degree] - rows[degree - 1]) / (NP * rows[degree])
    rows = legendre_rows(points, degree)
    weights = 2.0 / (degree * NP * rows[degree] ** 2)
    spacing = points[:, None] - points[None, :] + np.eye(NP)
    matrix = rows[degree][:, None] / rows[degree][None, :] / spacing
    corner = np.concatenate([[-degree * NP / 4.0], np.zeros(NP - 2), [degree * NP / 4.0]])
    matrix = matrix * (1.0 - np.eye(NP)) + np.eye(NP) * corner[None, :]
    unit = np.eye(NP)
    along_azim = np.kron(np.eye(2 * NP), matrix)
    along_span = np.kron(np.eye(2), np.kron(matrix, unit))
    along_radius = np.kron(matrix, np.eye(NP * NP))
    volume = np.kron(np.kron(weights, weights), weights).reshape(4, 1, LANES)
    volume = np.broadcast_to(volume, (4, ER, LANES)).reshape(16, LANES)
    return np.concatenate([along_azim.T, along_span.T], axis=1), along_radius.T, volume


def split(value):
    high = value.astype(BF16)
    return high, (value - high.astype(F32)).astype(BF16)


def dot(a, b):
    return jnp.dot(a, b, preferred_element_type=F32)


def dot_t(a, b):
    return lax.dot_general(a, b, (((1,), (1,)), ((), ())), preferred_element_type=F32)


def lane_of():
    return lax.broadcasted_iota(jnp.int32, (8, LANES), 1)


def sub_of():
    return lax.broadcasted_iota(jnp.int32, (8, LANES), 0)


def terms(vel, met, volume, tables, columns):
    ij2, ijl, kh, kl = tables
    wide = len(columns)
    n = wide * BLOCK
    first, last = columns[0], columns[-1] + 1
    if last - first == wide:
        take = lambda ref, c: ref[c, first * BLOCK : last * BLOCK, :]
    else:
        take = lambda ref, c: jnp.concatenate([ref[c, a * BLOCK : (a + 1) * BLOCK, :] for a in columns], axis=0)
    ext = [3.0 * take(vel, c) - 3.0 * take(vel, 3 + c) + take(vel, 6 + c) for c in range(3)]
    flat = jnp.concatenate(ext, axis=0)
    high, low = split(flat)
    both = jnp.concatenate([high, low], axis=1)
    s_ij = dot(both, ij2[...]) + dot(high, ijl[...])
    x = flat.reshape(3 * wide * 2, 2, 2, 8, LANES)
    one, two = x[:, 0], x[:, 1]
    bottom = (sub_of() < 4)[None, None]
    count = 3 * wide * 4

    def turn(v):
        return pltpu.roll(v.reshape(count, 8, LANES), 4, 1).reshape(v.shape)

    even = jnp.where(bottom, one, turn(two))
    odd = jnp.where(bottom, turn(one), two)
    lined = [w[:, m].reshape(count * 4, LANES) for m in range(2) for w in (even, odd)]
    lined = jnp.concatenate(lined, axis=1)
    khigh, klow = split(lined)
    s_k = dot(khigh, kh[...]) + dot(khigh, kl[...]) + dot(klow, kh[...])
    pieces = [s_k[:, LANES * t : LANES * (t + 1)].reshape(-1, 1, 8, LANES) for t in range(4)]
    even = jnp.concatenate([pieces[0], pieces[2]], axis=1)
    odd = jnp.concatenate([pieces[1], pieces[3]], axis=1)
    one = jnp.where(bottom, even, turn(odd))
    two = jnp.where(bottom, turn(even), odd)
    s_k = jnp.stack([one, two], axis=1).reshape(3 * n, LANES)
    m0, m1, m2 = (take(met, d) for d in range(3))
    volume = jnp.broadcast_to(volume[None], (wide * ES, 16, LANES)).reshape(n, LANES)
    mass = volume / (m0 * m1 * m2)
    a0, a1, a2 = ext[0] * m0, ext[1] * m1, ext[2] * m2
    out = []
    for c in range(3):
        part = slice(c * n, (c + 1) * n)
        conv = a0 * s_ij[part, :LANES] + a1 * s_ij[part, LANES:] + a2 * s_k[part]
        past = (3.0 / STEP_DT) * take(vel, c) - (1.5 / STEP_DT) * take(vel, 3 + c)
        past = past + (1.0 / (3.0 * STEP_DT)) * take(vel, 6 + c)
        out.append(mass * (past - conv))
    return out


def place_tables(ij_ref, k_ref, ij2, ijl, kh, kl):
    high, low = split(ij_ref[...])
    ij2[:LANES], ij2[LANES:], ijl[...] = high, high, low
    kh[...], kl[...] = split(k_ref[...])


def inner_sums(here):
    lane, sub = lane_of(), sub_of()
    j_of = lane // 8 % 8
    k_down = (lane < 64) & (sub >= 1) & (sub < 4)
    k_up = (lane >= 64) & (sub >= 4) & (sub < 7)
    gap = jnp.zeros((2, 8, LANES), F32)
    down = pltpu.roll(jnp.where(j_of == 0, here[2:], 0.0), 56, 2)
    up = pltpu.roll(jnp.where(j_of == 7, here[:-2], 0.0), LANES - 56, 2)
    here = here + jnp.concatenate([down, gap], axis=0) + jnp.concatenate([gap, up], axis=0)
    pairs = here.reshape(ES, 2, 8, LANES)
    inner, outer = pairs[:, 0], pairs[:, 1]
    from_above = pltpu.roll(pltpu.roll(inner, 64, 2), 3, 1)
    from_below = pltpu.roll(pltpu.roll(outer, 64, 2), 5, 1)
    inner = inner + jnp.where(k_down, from_below, 0.0)
    outer = outer + jnp.where(k_up, from_above, 0.0)
    return jnp.stack([inner, outer], axis=1)


def traces(vel, tab_ref, face_ref, side_ref, slot_ref, off_ref):
    last = pl.ds(15, SLOTS, stride=16)
    faces = [3.0 * vel[c, last, :] - 3.0 * vel[3 + c, last, :] + vel[6 + c, last, :] for c in range(3)]
    faces = jnp.concatenate(faces, axis=0)[:, 64:]
    table = tab_ref[...].reshape(NOFF * 64, 64)
    fh, fl = split(faces)
    th, tl = split(table)
    every = dot_t(fh, th) + dot_t(fh, tl) + dot_t(fl, th)
    side = side_ref[...]
    target = jnp.where(side >= 0, side * SLOTS + slot_ref[...], -1)
    hit_t = (lax.broadcasted_iota(jnp.int32, (2 * SLOTS, TL), 0) == target).astype(BF16)
    combo = off_ref[...] * SLOTS + face_ref[...]
    hit_c = (lax.broadcasted_iota(jnp.int32, (NOFF * SLOTS, TL), 0) == combo).astype(BF16)
    counts = dot_t(hit_t, hit_c).astype(BF16)
    left = (lane_of() < 64)[:1]
    zero = jnp.zeros((SLOTS, LANES), F32)
    stacked = []
    for pair in range(NOFF // 2):
        r0, r1, r2 = (every[c * SLOTS : (c + 1) * SLOTS, pair * LANES : (pair + 1) * LANES] for c in range(3))
        t0, t1, t2 = (pltpu.roll(v, 64, 1) for v in (r0, r1, r2))
        stacked.append(jnp.concatenate([jnp.where(left, r0, t1), jnp.where(left, r2, zero)], axis=1))
        stacked.append(jnp.concatenate([jnp.where(left, t0, r1), jnp.where(left, t2, zero)], axis=1))
    stacked = jnp.concatenate(stacked, axis=0)
    sh, sl = split(stacked)
    return dot(counts, sh) + dot(counts, sl)


def rim_kernel(
    place, face_ref, side_ref, slot_ref, off_ref, vel_hbm, met_hbm, tab_hbm, ij_hbm, k_hbm, vol_hbm,
    vel, met, ij_ref, k_ref, vol_ref, rim_ref, e_ref, o_ref, own_ref, tab_ref, ij2, ijl, kh, kl, sem,
):
    ends, middle = (pl.ds(0, BLOCK), pl.ds((EA - 1) * BLOCK, BLOCK)), pl.ds(BLOCK, (EA - 2) * BLOCK)
    moves = [(vel_hbm.at[:, part], vel.at[:, part]) for part in ends] + [(ij_hbm, ij_ref), (k_hbm, k_ref)]
    moves += [(met_hbm.at[:, part], met.at[:, part]) for part in ends] + [(vol_hbm, vol_ref), (tab_hbm, tab_ref)]
    moves += [(vel_hbm.at[:, middle], vel.at[:, middle]), (met_hbm.at[:, middle], met.at[:, middle])]
    copies = [pltpu.make_async_copy(source, target, sem.at[q]) for q, (source, target) in enumerate(moves)]
    for copy in copies:
        copy.start()
    for copy in copies[:7]:
        copy.wait()
    place_tables(ij_ref, k_ref, ij2, ijl, kh, kl)
    raw = terms(vel, met, vol_ref[...], (ij2, ijl, kh, kl), (0, EA - 1))
    lane = lane_of()
    faces = [[], []]
    for c in range(3):
        for end in range(2):
            column = raw[c][end * BLOCK : (end + 1) * BLOCK]
            rim_ref[c, end] = column
            here = inner_sums(column.reshape(8, 8, LANES))
            keep = lane % 8 == 7 * end
            face = jnp.zeros((8, LANES), F32)
            for m in range(8):
                face += pltpu.roll(jnp.where(keep, here[m // 2, m % 2], 0.0), (m - 7 * end) % LANES, 1)
            faces[end].append(face)
    low, high = jnp.concatenate(faces[0], axis=0), jnp.concatenate(faces[1], axis=0)
    is_odd = place[0] == 1
    e_ref[:24, :] = jnp.where(is_odd, low, high)
    o_ref[:24, :] = jnp.where(is_odd, high, low)
    for copy in copies[7:]:
        copy.wait()
    trace = traces(vel, tab_ref, face_ref, side_ref, slot_ref, off_ref)
    own_ref[...] = trace[:SLOTS]
    packed = jnp.concatenate([trace[SLOTS:, :LANES], trace[SLOTS:, LANES:]], axis=0)
    e_ref[24:, :] = packed
    o_ref[24:, :] = packed


def rest_kernel(vel, met, ij_ref, k_ref, vol_ref, rim_ref, out_ref, span_ref, total, ij2, ijl, kh, kl):
    place_tables(ij_ref, k_ref, ij2, ijl, kh, kl)
    for c in range(3):
        total[c, :BLOCK] = rim_ref[c, 0]
        total[c, (EA - 1) * BLOCK :] = rim_ref[c, 1]
    step = (EA - 2) // CHUNKS
    for q in range(CHUNKS):
        columns = tuple(range(1 + q * step, 1 + (q + 1) * step))
        for c, part in enumerate(terms(vel, met, vol_ref[...], (ij2, ijl, kh, kl), columns)):
            total[c, columns[0] * BLOCK : (columns[-1] + 1) * BLOCK] = part
    lane = lane_of()
    i_of, j_of = lane % 8, lane // 8 % 8
    span_faces = [[jnp.zeros((2, 8, LANES), F32) for c in range(3)] for end in range(2)]
    for c in range(3):
        for a in range(EA):
            here = total[c, pl.ds(a * BLOCK, BLOCK), :].reshape(8, 8, LANES)
            if a < EA - 1:
                above = total[c, pl.ds((a + 1) * BLOCK, BLOCK), :].reshape(8, 8, LANES)
                here = here + pltpu.roll(jnp.where(i_of == 0, above, 0.0), 7, 2)
            if a > 0:
                below = total[c, pl.ds((a - 1) * BLOCK, BLOCK), :].reshape(8, 8, LANES)
                here = here + pltpu.roll(jnp.where(i_of == 7, below, 0.0), LANES - 7, 2)
            here = inner_sums(here)
            out_ref[c, pl.ds(a * BLOCK, BLOCK), :] = here.reshape(BLOCK, LANES)
            for end in range(2):
                face = jnp.where(j_of == 7 * end, here[3 * end], 0.0)
                span_faces[end][c] += pltpu.roll(face, (8 * a - 56 * end) % LANES, 2)
    for end in range(2):
        span_ref[end] = jnp.concatenate([f.reshape(16, LANES) for f in span_faces[end]], axis=0)


def corner_kernel(parity, e_ref, o_ref, span_ref, own_ref, se_ref, so_ref, low_ref, high_ref, sum_ref):
    is_odd = parity[0] == 1
    from_e, from_o = e_ref[...], o_ref[...]
    low = jnp.where(is_odd, from_e, from_o)
    high = jnp.where(is_odd, from_o, from_e)
    low_ref[...] = low[:24]
    high_ref[...] = high[:24]
    arrived = low[24:]
    sum_ref[...] = own_ref[...] + jnp.concatenate([arrived[:SLOTS], arrived[SLOTS:]], axis=1)
    half = lane_of() % 64
    ends = []
    for end in range(2):
        parts = []
        for c in range(3):
            for t in range(2):
                face = span_ref[end, pl.ds((c * 2 + t) * 8, 8), :]
                m = 6 * end + t
                seat = m + 56 * end
                face += jnp.where(half == 0, pltpu.roll(low[c * 8 : c * 8 + 8], -seat % LANES, 1), 0.0)
                face += jnp.where(half == 63, pltpu.roll(high[c * 8 : c * 8 + 8], (63 - seat) % LANES, 1), 0.0)
                parts.append(face)
        ends.append(jnp.concatenate(parts, axis=0))
    odd = parity[1] == 1
    se_ref[...] = jnp.where(odd, ends[0], ends[1])
    so_ref[...] = jnp.where(odd, ends[1], ends[0])


def final_kernel(place, part_ref, low_ref, high_ref, se_ref, so_ref, out_hbm, work, sem):
    inner = [pl.ds(a * BLOCK + 16, 32) for a in range(1, EA - 1)]
    outer = [pl.ds(0, BLOCK + 16)] + [pl.ds(a * BLOCK + 48, 32) for a in range(1, EA - 2)]
    outer += [pl.ds((EA - 1) * BLOCK - 16, BLOCK + 16)]
    copies = [pltpu.make_async_copy(part_ref.at[:, r], out_hbm.at[:, r], sem.at[q]) for q, r in enumerate(inner)]
    for copy in copies:
        copy.start()
    odd = place[1] == 1
    from_e, from_o = se_ref[...], so_ref[...]
    span_low = jnp.where(odd, from_e, from_o) * jnp.where(place[2] == 0, 0.0, 1.0)
    span_high = jnp.where(odd, from_o, from_e) * jnp.where(place[2] == 1, 0.0, 1.0)
    lane = lane_of()
    i_of, j_of = lane % 8, lane // 8 % 8
    for a in range(EA):
        for c in range(3):
            for m in range(8):
                end_s = {0: 0, 3: 1}.get(m // 2)
                end_a = {0: 0, EA - 1: 1}.get(a)
                if end_s is None and end_a is None:
                    continue
                rows = pl.ds(a * BLOCK + 8 * m, 8)
                here = part_ref[c, rows, :]
                if end_a is not None:
                    face = (low_ref, high_ref)[end_a][pl.ds(c * 8, 8), :]
                    here += jnp.where(i_of == 7 * end_a, pltpu.roll(face, (7 * end_a - m) % LANES, 1), 0.0)
                if end_s is not None:
                    base = (c * 2 + m % 2) * 8
                    face = (span_low, span_high)[end_s][base : base + 8]
                    here += jnp.where(j_of == 7 * end_s, pltpu.roll(face, (56 * end_s - 8 * a) % LANES, 1), 0.0)
                work[c, rows, :] = here
        if a >= 1:
            q = a - 1
            r = outer[q]
            copy = pltpu.make_async_copy(work.at[:, r], out_hbm.at[:, r], sem.at[len(inner) + q])
            copy.start()
            copies.append(copy)
    for copy in copies:
        copy.wait()


def swap(value, axis, first):
    count = lax.axis_size(axis)
    pairs = []
    for low in range(first, count + first, 2):
        pairs += [(low % count, (low + 1) % count), ((low + 1) % count, low % count)]
    return lax.ppermute(value, axis, pairs)


def turned(value, by):
    count = lax.axis_size("azim")
    return lax.ppermute(value, "azim", [(i, (i + by) % count) for i in range(count)])


def local(velocity, metric, mortar_tables, angle_step, tile_face, tile_side, tile_slot, tile_offset):
    d_ij, d_k, volume = spectral_tables()
    azim, span = lax.axis_index("azim"), lax.axis_index("span")
    edge = jnp.where(span == 0, 0, jnp.where(span == lax.axis_size("span") - 1, 1, 2))
    place = jnp.stack([azim % 2, span % 2, edge]).astype(jnp.int32)
    vel = velocity.reshape(9, EA * ES, ER, 4, LANES).transpose(0, 1, 3, 2, 4).reshape(9, ROWS, LANES)
    met = metric.reshape(3, EA * ES, ER, 4, LANES).transpose(0, 1, 3, 2, 4).reshape(3, ROWS, LANES)
    smem = pl.BlockSpec(memory_space=pltpu.SMEM)
    vmem = pl.BlockSpec(memory_space=pltpu.VMEM)
    hbm = pl.BlockSpec(memory_space=pltpu.HBM)
    f = lambda *shape: jax.ShapeDtypeStruct(shape, F32)
    v = lambda *shape: pltpu.VMEM(shape, F32)
    far = lambda x: pltpu.with_memory_space_constraint(x, pltpu.HBM)
    lists = [t.reshape(1, TL) for t in (tile_face, tile_side, tile_slot, tile_offset)]
    bf16_tables = [
        pltpu.VMEM((256, 256), BF16), pltpu.VMEM((128, 256), BF16), pltpu.VMEM((512, 512), BF16), pltpu.VMEM((512, 512), BF16)
    ]
    vel_v, met_v, ij_v, k_v, vol_v, rim, to_e, to_o, own = pl.pallas_call(
        rim_kernel,
        out_shape=(
            v(9, ROWS, LANES), v(3, ROWS, LANES), v(LANES, 256), v(512, 512), v(16, LANES), v(3, 2, BLOCK, LANES),
            v(88, LANES), v(88, LANES), v(SLOTS, 2 * LANES),
        ),
        in_specs=[smem] + [vmem] * 4 + [hbm] * 6,
        out_specs=[vmem] * 9,
        scratch_shapes=[pltpu.VMEM((NOFF, 64, 64), F32)] + bf16_tables + [pltpu.SemaphoreType.DMA((10,))],
        compiler_params=pltpu.CompilerParams(vmem_limit_bytes=LIMIT),
        name="rim_terms",
    )(
        place, *lists, far(vel), far(met), far(mortar_tables), far(jnp.asarray(d_ij, F32)), far(jnp.asarray(d_k, F32)),
        far(jnp.asarray(volume, F32)),
    )
    from_e = swap(to_e, "azim", 0)
    from_o = swap(to_o, "azim", 1)
    part, span_faces = pl.pallas_call(
        rest_kernel,
        out_shape=(v(3, ROWS, LANES), v(2, 48, LANES)),
        in_specs=[vmem] * 6,
        out_specs=[vmem] * 2,
        scratch_shapes=[pltpu.VMEM((3, ROWS, LANES), F32)] + bf16_tables,
        compiler_params=pltpu.CompilerParams(vmem_limit_bytes=LIMIT),
        cost_estimate=pl.CostEstimate(flops=10**9, bytes_accessed=8 * 2**20, transcendentals=0),
        name="rest_terms",
    )(vel_v, met_v, ij_v, k_v, vol_v, rim)
    to_se, to_so, low, high, summed = pl.pallas_call(
        corner_kernel,
        out_shape=(v(48, LANES), v(48, LANES), v(24, LANES), v(24, LANES), v(SLOTS, 2 * LANES)),
        in_specs=[smem] + [vmem] * 4,
        out_specs=[vmem] * 5,
        name="corners",
    )(place, from_e, from_o, span_faces, own)
    from_se = swap(to_se, "span", 0)
    from_so = swap(to_so, "span", 1)
    count = lax.axis_size("azim")
    trace = lax.switch(angle_step[0] % count, [lambda v, k=k: turned(v, k) for k in range(count)], summed)
    rhs = pl.pallas_call(
        final_kernel,
        out_shape=f(3, ROWS, LANES),
        in_specs=[smem] + [vmem] * 5,
        out_specs=hbm,
        scratch_shapes=[pltpu.VMEM((3, ROWS, LANES), F32), pltpu.SemaphoreType.DMA((13,))],
        name="join",
    )(place, part, low, high, from_se, from_so)
    rhs = rhs.reshape(3, EA * ES, 4, ER, LANES).transpose(0, 1, 3, 2, 4).reshape(3, EA, ES, ER, 4 * LANES)
    stator = trace[:, :192].reshape(SLOTS, 3, 64)
    return rhs, stator


def solution(mesh):
    return jax.shard_map(
        local,
        mesh=mesh,
        in_specs=(
            P(None, None, "azim", "span", None, None),
            P(None, "azim", "span", None, None),
            P(),
            P(),
            P("azim", "span", None),
            P("azim", "span", None),
            P("azim", "span", None),
            P("azim", "span", None),
        ),
        out_specs=(P(None, "azim", "span", None, None), P(("azim", "span"), None, None)),
        check_vma=False,
    )
```

```python
import jax
import jax.numpy as jnp
import numpy as np
from jax import lax
from jax.experimental import pallas as pl
from jax.experimental.pallas import tpu as pltpu
from jax.sharding import PartitionSpec as P

NP = 8
STEP_DT = 0.05
EA, ES, ER = 8, 4, 4
BLOCK = ES * 16
ROWS = EA * BLOCK
LANES = 128
TL = 64
NOFF = 8
SLOTS = 32
WIDE = 3
F32 = jnp.float32
BF16 = jnp.bfloat16


def legendre_rows(points, degree):
    rows = [points * 0.0 + 1.0, points]
    for level in range(2, degree + 1):
        rows.append(((2 * level - 1) * points * rows[-1] - (level - 1) * rows[-2]) / level)
    return rows


def spectral_tables():
    degree = NP - 1
    points = -np.cos(np.pi * np.arange(NP) / degree)
    for newton_step in range(60):
        rows = legendre_rows(points, degree)
        points = points - (points * rows[degree] - rows[degree - 1]) / (NP * rows[degree])
    rows = legendre_rows(points, degree)
    weights = 2.0 / (degree * NP * rows[degree] ** 2)
    spacing = points[:, None] - points[None, :] + np.eye(NP)
    matrix = rows[degree][:, None] / rows[degree][None, :] / spacing
    corner = np.concatenate([[-degree * NP / 4.0], np.zeros(NP - 2), [degree * NP / 4.0]])
    matrix = matrix * (1.0 - np.eye(NP)) + np.eye(NP) * corner[None, :]
    unit = np.eye(NP)
    along_azim = np.kron(np.eye(2 * NP), matrix)
    along_span = np.kron(np.eye(2), np.kron(matrix, unit))
    volume = np.kron(np.kron(weights, weights), weights).reshape(4, 1, LANES)
    volume = np.broadcast_to(volume, (4, ER, LANES)).reshape(16, LANES)
    sub, lane = np.arange(8)[:, None], np.arange(LANES)[None, :]
    half, side = sub // 4, lane // 64
    radial = []
    for out in range(2):
        for m in range(2):
            for p in range(2):
                for q in range(2):
                    to = 2 * (2 * out + half) + side
                    source = 2 * (2 * m + half * (1 - p) + (1 - half) * p) + side * (1 - q) + (1 - side) * q
                    radial.append(matrix[to, source])
    return np.concatenate([along_azim.T, along_span.T] + radial + [volume], axis=0)


def split(value):
    high = value.astype(BF16)
    return high, (value - high.astype(F32)).astype(BF16)


def dot(a, b):
    return jnp.dot(a, b, preferred_element_type=F32)


def dot_t(a, b):
    return lax.dot_general(a, b, (((1,), (1,)), ((), ())), preferred_element_type=F32)


def lane_of():
    return lax.broadcasted_iota(jnp.int32, (8, LANES), 1)


def sub_of():
    return lax.broadcasted_iota(jnp.int32, (8, LANES), 0)


def terms(take, tab_ref, ij2, ijl):
    ext = [3.0 * take(0, c) - 3.0 * take(0, 3 + c) + take(0, 6 + c) for c in range(3)]
    n = ext[0].shape[0]
    high, low = split(jnp.concatenate(ext, axis=0))
    s_ij = dot(jnp.concatenate([high, low], axis=1), ij2[...]) + dot(high, ijl[...])
    m0, m1, m2 = (take(1, d) for d in range(3))
    volume = jnp.broadcast_to(tab_ref[384:, :][None], (n // 16, 16, LANES)).reshape(n, LANES)
    mass = volume / (m0 * m1 * m2)
    a0, a1, a2 = ext[0] * m0, ext[1] * m1, ext[2] * m2
    out = []
    for c in range(3):
        part = slice(c * n, (c + 1) * n)
        pairs = ext[c].reshape(n // 16, 2, 8, LANES)
        seen = []
        for m in range(2):
            for v in (pairs[:, m], pltpu.roll(pairs[:, m], 4, 1)):
                seen += [v, pltpu.roll(v, 64, 2)]
        s_k = []
        for o in range(2):
            s_k.append(sum(v * tab_ref[256 + 64 * o + 8 * q : 264 + 64 * o + 8 * q, :] for q, v in enumerate(seen)))
        s_k = jnp.stack(s_k, axis=1).reshape(n, LANES)
        conv = a0 * s_ij[part, :LANES] + a1 * s_ij[part, LANES:] + a2 * s_k
        past = (3.0 / STEP_DT) * take(0, c) - (1.5 / STEP_DT) * take(0, 3 + c)
        past = past + (1.0 / (3.0 * STEP_DT)) * take(0, 6 + c)
        out.append(mass * (past - conv))
    return out


def place_tables(tab_ref, ij2, ijl):
    high, low = split(jnp.concatenate([tab_ref[:LANES, :], tab_ref[LANES : 2 * LANES, :]], axis=1))
    ij2[:LANES, :], ij2[LANES:, :], ijl[...] = high, high, low


def inner_sums(here):
    lane, sub = lane_of(), sub_of()
    j_of = lane // 8 % 8
    k_down = (lane < 64) & (sub >= 1) & (sub < 4)
    k_up = (lane >= 64) & (sub >= 4) & (sub < 7)
    gap = jnp.zeros((2, 8, LANES), F32)
    down = pltpu.roll(jnp.where(j_of == 0, here[2:], 0.0), 56, 2)
    up = pltpu.roll(jnp.where(j_of == 7, here[:-2], 0.0), LANES - 56, 2)
    here = here + jnp.concatenate([down, gap], axis=0) + jnp.concatenate([gap, up], axis=0)
    pairs = here.reshape(ES, 2, 8, LANES)
    inner, outer = pairs[:, 0], pairs[:, 1]
    from_above = pltpu.roll(pltpu.roll(inner, 64, 2), 3, 1)
    from_below = pltpu.roll(pltpu.roll(outer, 64, 2), 5, 1)
    inner = inner + jnp.where(k_down, from_below, 0.0)
    outer = outer + jnp.where(k_up, from_above, 0.0)
    return jnp.stack([inner, outer], axis=1)


def traces(vel, tab_ref, face_ref, side_ref, slot_ref, off_ref):
    last = pl.ds(15, SLOTS, stride=16)
    faces = [3.0 * vel[c, last, :] - 3.0 * vel[3 + c, last, :] + vel[6 + c, last, :] for c in range(3)]
    faces = jnp.concatenate(faces, axis=0)[:, 64:]
    table = tab_ref[...].reshape(NOFF * 64, 64)
    fh, fl = split(faces)
    th, tl = split(table)
    every = dot_t(fh, th) + dot_t(fh, tl) + dot_t(fl, th)
    side = side_ref[...]
    target = jnp.where(side >= 0, side * SLOTS + slot_ref[...], -1)
    hit_t = (lax.broadcasted_iota(jnp.int32, (2 * SLOTS, TL), 0) == target).astype(BF16)
    combo = off_ref[...] * SLOTS + face_ref[...]
    hit_c = (lax.broadcasted_iota(jnp.int32, (NOFF * SLOTS, TL), 0) == combo).astype(BF16)
    counts = dot_t(hit_t, hit_c).astype(BF16)
    left = (lane_of() < 64)[:1]
    zero = jnp.zeros((SLOTS, LANES), F32)
    stacked = []
    for pair in range(NOFF // 2):
        r0, r1, r2 = (every[c * SLOTS : (c + 1) * SLOTS, pair * LANES : (pair + 1) * LANES] for c in range(3))
        t0, t1, t2 = (pltpu.roll(v, 64, 1) for v in (r0, r1, r2))
        stacked.append(jnp.concatenate([jnp.where(left, r0, t1), jnp.where(left, r2, zero)], axis=1))
        stacked.append(jnp.concatenate([jnp.where(left, t0, r1), jnp.where(left, t2, zero)], axis=1))
    stacked = jnp.concatenate(stacked, axis=0)
    sh, sl = split(stacked)
    return dot(counts, sh) + dot(counts, sl)


def rim_kernel(
    face_hbm, side_hbm, slot_hbm, off_hbm, vel_hbm, met_hbm, mortar_hbm, tab_hbm,
    vel, met, tab_ref, rim_ref, e_ref, o_ref, own_ref, mortar, face_ref, side_ref, slot_ref, off_ref, ij2, ijl, sem,
):
    ends, middle = (pl.ds(0, BLOCK), pl.ds((EA - 1) * BLOCK, BLOCK)), pl.ds(BLOCK, (EA - 2) * BLOCK)
    moves = [(tab_hbm, tab_ref)] + [(vel_hbm.at[:, part], vel.at[:, part]) for part in ends]
    moves += [(met_hbm.at[:, part], met.at[:, part]) for part in ends]
    moves += [(vel_hbm.at[:, middle], vel.at[:, middle]), (mortar_hbm, mortar)]
    moves += [(face_hbm, face_ref), (side_hbm, side_ref), (slot_hbm, slot_ref), (off_hbm, off_ref)]
    moves += [(met_hbm.at[:, middle], met.at[:, middle])]
    copies = [pltpu.make_async_copy(source, target, sem.at[q]) for q, (source, target) in enumerate(moves)]
    for copy in copies:
        copy.start()
    is_odd = lax.axis_index("azim") % 2 == 1
    copies[0].wait()
    place_tables(tab_ref, ij2, ijl)
    for copy in copies[1:5]:
        copy.wait()

    def take(kind, q):
        ref = (vel, met)[kind]
        return jnp.concatenate([ref[q, :BLOCK, :], ref[q, (EA - 1) * BLOCK :, :]], axis=0)

    raw = terms(take, tab_ref, ij2, ijl)
    lane = lane_of()
    faces = [[], []]
    for c in range(3):
        for end in range(2):
            column = raw[c][end * BLOCK : (end + 1) * BLOCK]
            rim_ref[c, end] = column
            here = inner_sums(column.reshape(8, 8, LANES))
            keep = lane % 8 == 7 * end
            face = jnp.zeros((8, LANES), F32)
            for m in range(8):
                face += pltpu.roll(jnp.where(keep, here[m // 2, m % 2], 0.0), (m - 7 * end) % LANES, 1)
            faces[end].append(face)
    low, high = jnp.concatenate(faces[0], axis=0), jnp.concatenate(faces[1], axis=0)
    e_ref[:24, :] = jnp.where(is_odd, low, high)
    o_ref[:24, :] = jnp.where(is_odd, high, low)
    for copy in copies[5:]:
        copy.wait()
    trace = traces(vel, mortar, face_ref, side_ref, slot_ref, off_ref)
    own_ref[...] = trace[:SLOTS]
    packed = jnp.concatenate([trace[SLOTS:, :LANES], trace[SLOTS:, LANES:]], axis=0)
    e_ref[24:, :] = packed
    o_ref[24:, :] = packed


def rest_kernel(vel, met, tab_ref, rim_ref, out_ref, span_ref, total, ij2, ijl):
    place_tables(tab_ref, ij2, ijl)
    for c in range(3):
        total[c, 0] = jnp.zeros((BLOCK, LANES), F32)
        total[c, EA + 1] = jnp.zeros((BLOCK, LANES), F32)
        total[c, 1] = rim_ref[c, 0]
        total[c, EA] = rim_ref[c, 1]
    span_ref[...] = jnp.zeros_like(span_ref)

    @pl.loop(0, (EA - 2) // WIDE)
    def _(q):
        first = 1 + q * WIDE
        rows = pl.ds(pl.multiple_of(first * BLOCK, BLOCK), WIDE * BLOCK)
        raw = terms(lambda kind, d: (vel, met)[kind][d, rows, :], tab_ref, ij2, ijl)
        for c, part in enumerate(raw):
            total[c, pl.ds(first + 1, WIDE)] = part.reshape(WIDE, BLOCK, LANES)

    lane = lane_of()
    i_of, j_of = lane % 8, lane // 8 % 8

    @pl.loop(0, EA, unroll=2)
    def _(a):
        for c in range(3):
            here, below, above = (total[c, a + d].reshape(8, 8, LANES) for d in (1, 0, 2))
            here = here + pltpu.roll(jnp.where((i_of == 0) & (a < EA - 1), above, 0.0), 7, 2)
            here = here + pltpu.roll(jnp.where((i_of == 7) & (a > 0), below, 0.0), LANES - 7, 2)
            here = inner_sums(here)
            out_ref[c, a] = here.reshape(BLOCK, LANES)
            for end in range(2):
                face = jnp.where(j_of == 7 * end, here[3 * end], 0.0)
                shift = lax.rem(8 * a + LANES - 56 * end, LANES)
                for t in range(2):
                    rows = pl.ds((c * 2 + t) * 8, 8)
                    span_ref[end, rows, :] += pltpu.roll(face[t], shift, 1)


def corner_kernel(e_ref, o_ref, span_ref, own_ref, se_ref, so_ref, low_ref, high_ref, sum_ref):
    is_odd = lax.axis_index("azim") % 2 == 1
    from_e, from_o = e_ref[...], o_ref[...]
    low = jnp.where(is_odd, from_e, from_o)
    high = jnp.where(is_odd, from_o, from_e)
    low_ref[...] = low[:24]
    high_ref[...] = high[:24]
    arrived = low[24:]
    sum_ref[...] = own_ref[...] + jnp.concatenate([arrived[:SLOTS], arrived[SLOTS:]], axis=1)
    half = lane_of() % 64
    ends = []
    for end in range(2):
        parts = []
        for c in range(3):
            for t in range(2):
                face = span_ref[end, pl.ds((c * 2 + t) * 8, 8), :]
                m = 6 * end + t
                seat = m + 56 * end
                face += jnp.where(half == 0, pltpu.roll(low[c * 8 : c * 8 + 8], -seat % LANES, 1), 0.0)
                face += jnp.where(half == 63, pltpu.roll(high[c * 8 : c * 8 + 8], (63 - seat) % LANES, 1), 0.0)
                parts.append(face)
        ends.append(jnp.concatenate(parts, axis=0))
    odd = lax.axis_index("span") % 2 == 1
    se_ref[...] = jnp.where(odd, ends[0], ends[1])
    so_ref[...] = jnp.where(odd, ends[1], ends[0])


def final_kernel(part_ref, low_ref, high_ref, se_ref, so_ref, out_hbm, work, span_faces, sem):
    middle = pl.ds(1, EA - 2)
    spots = ((middle, pl.ds(16, 32)), (0, pl.ds(0, BLOCK)), (EA - 1, pl.ds(0, BLOCK)), (middle, pl.ds(0, 16)), (middle, pl.ds(48, 16)))
    copies = [
        pltpu.make_async_copy((work if q else part_ref).at[:, a, r], out_hbm.at[:, a, r], sem.at[q]) for q, (a, r) in enumerate(spots)
    ]
    copies[0].start()
    span = lax.axis_index("span")
    odd = span % 2 == 1
    from_e, from_o = se_ref[...], so_ref[...]
    span_faces[0] = jnp.where(span == 0, 0.0, jnp.where(odd, from_e, from_o))
    span_faces[1] = jnp.where(span == lax.axis_size("span") - 1, 0.0, jnp.where(odd, from_o, from_e))
    lane = lane_of()
    i_of, j_of = lane % 8, lane // 8 % 8

    @pl.loop(0, 8, unroll=4)
    def _(m):
        rows = pl.ds(pl.multiple_of(8 * m, 8), 8)
        for end, ref in enumerate((low_ref, high_ref)):
            for c in range(3):
                face = pltpu.roll(ref[8 * c : 8 * c + 8, :], lax.rem(7 * end + LANES - m, LANES), 1)
                work[c, (EA - 1) * end, rows, :] = part_ref[c, (EA - 1) * end, rows, :] + jnp.where(i_of == 7 * end, face, 0.0)

    def edges(a, source):
        for end in range(2):
            for c in range(3):
                for t in range(2):
                    rows = pl.ds(48 * end + 8 * t, 8)
                    face = span_faces[end, (c * 2 + t) * 8 : (c * 2 + t) * 8 + 8, :]
                    face = pltpu.roll(face, lax.rem(56 * end + LANES - 8 * a, LANES), 1)
                    work[c, a, rows, :] = source[c, a, rows, :] + jnp.where(j_of == 7 * end, face, 0.0)

    for q, a in ((1, 0), (2, EA - 1)):
        edges(a, work)
        copies[q].start()

    @pl.loop(1, EA - 1, unroll=6)
    def _(a):
        edges(a, part_ref)

    copies[3].start()
    copies[4].start()
    for copy in copies:
        copy.wait()


def swap(value, axis, first):
    count = lax.axis_size(axis)
    pairs = []
    for low in range(first, count + first, 2):
        pairs += [(low % count, (low + 1) % count), ((low + 1) % count, low % count)]
    return lax.ppermute(value, axis, pairs)


def turned(value, by):
    count = lax.axis_size("azim")
    return lax.ppermute(value, "azim", [(i, (i + by) % count) for i in range(count)])


def local(velocity, metric, mortar_tables, angle_step, tile_face, tile_side, tile_slot, tile_offset):
    vel = velocity.reshape(9, EA * ES, ER, 4, LANES).transpose(0, 1, 3, 2, 4).reshape(9, ROWS, LANES)
    met = metric.reshape(3, EA * ES, ER, 4, LANES).transpose(0, 1, 3, 2, 4).reshape(3, ROWS, LANES)
    vmem = pl.BlockSpec(memory_space=pltpu.VMEM)
    hbm = pl.BlockSpec(memory_space=pltpu.HBM)
    v = lambda *shape: pltpu.VMEM(shape, F32)
    far = lambda x: pltpu.with_memory_space_constraint(x, pltpu.HBM)
    limit = lambda mib: pltpu.CompilerParams(vmem_limit_bytes=mib * 2**20)
    lists = [far(t.reshape(1, TL)) for t in (tile_face, tile_side, tile_slot, tile_offset)]
    bf16_tables = [pltpu.VMEM((256, 256), BF16), pltpu.VMEM((128, 256), BF16)]
    vel_v, met_v, tab_v, rim, to_e, to_o, own = pl.pallas_call(
        rim_kernel,
        out_shape=(
            v(9, ROWS, LANES), v(3, ROWS, LANES), v(400, LANES), v(3, 2, BLOCK, LANES), v(88, LANES), v(88, LANES), v(SLOTS, 2 * LANES)
        ),
        in_specs=[hbm] * 8,
        out_specs=[vmem] * 7,
        scratch_shapes=[pltpu.VMEM((NOFF, 64, 64), F32)]
        + [pltpu.VMEM((1, TL), jnp.int32)] * 4
        + bf16_tables
        + [pltpu.SemaphoreType.DMA((12,))],
        compiler_params=limit(24),
        name="rim_terms",
    )(*lists, far(vel), far(met), far(mortar_tables), far(jnp.asarray(spectral_tables(), F32)))
    from_e = swap(to_e, "azim", 0)
    from_o = swap(to_o, "azim", 1)
    part, span_faces = pl.pallas_call(
        rest_kernel,
        out_shape=(v(3, EA, BLOCK, LANES), v(2, 48, LANES)),
        in_specs=[vmem] * 4,
        out_specs=[vmem] * 2,
        scratch_shapes=[pltpu.VMEM((3, EA + 2, BLOCK, LANES), F32)] + bf16_tables,
        compiler_params=limit(24),
        cost_estimate=pl.CostEstimate(flops=10**9, bytes_accessed=8 * 2**20, transcendentals=0),
        name="rest_terms",
    )(vel_v, met_v, tab_v, rim)
    to_se, to_so, low, high, summed = pl.pallas_call(
        corner_kernel,
        out_shape=(v(48, LANES), v(48, LANES), v(24, LANES), v(24, LANES), v(SLOTS, 2 * LANES)),
        in_specs=[vmem] * 4,
        out_specs=[vmem] * 5,
        compiler_params=limit(8),
        name="corners",
    )(from_e, from_o, span_faces, own)
    from_se = swap(to_se, "span", 0)
    from_so = swap(to_so, "span", 1)
    count = lax.axis_size("azim")
    trace = lax.switch(angle_step[0] % count, [lambda v, k=k: turned(v, k) for k in range(count)], summed)
    rhs = pl.pallas_call(
        final_kernel,
        out_shape=jax.ShapeDtypeStruct((3, EA, BLOCK, LANES), F32),
        in_specs=[vmem] * 5,
        out_specs=hbm,
        scratch_shapes=[
            pltpu.VMEM((3, EA, BLOCK, LANES), F32), pltpu.VMEM((2, 48, LANES), F32), pltpu.SemaphoreType.DMA((5,))
        ],
        compiler_params=limit(8),
        name="join",
    )(part, low, high, from_se, from_so)
    rhs = rhs.reshape(3, EA * ES, 4, ER, LANES).transpose(0, 1, 3, 2, 4).reshape(3, EA, ES, ER, 4 * LANES)
    stator = trace[:, :192].reshape(SLOTS, 3, 64)
    return rhs, stator


def solution(mesh):
    return jax.shard_map(
        local,
        mesh=mesh,
        in_specs=(
            P(None, None, "azim", "span", None, None),
            P(None, "azim", "span", None, None),
            P(),
            P(),
            P("azim", "span", None),
            P("azim", "span", None),
            P("azim", "span", None),
            P("azim", "span", None),
        ),
        out_specs=(P(None, "azim", "span", None, None), P(("azim", "span"), None, None)),
        check_vma=False,
    )
```

```python
import jax
import jax.numpy as jnp
import numpy as np
from jax import lax
from jax.experimental import pallas as pl
from jax.experimental.pallas import tpu as pltpu
from jax.sharding import PartitionSpec as P

NP = 8
STEP_DT = 0.05
EA, ES, ER = 8, 4, 4
BLOCK = ES * 16
ROWS = EA * BLOCK
LANES = 128
TL = 64
NOFF = 8
SLOTS = 32
WIDE = 3
F32 = jnp.float32
BF16 = jnp.bfloat16


def legendre_rows(points, degree):
    rows = [points * 0.0 + 1.0, points]
    for level in range(2, degree + 1):
        rows.append(((2 * level - 1) * points * rows[-1] - (level - 1) * rows[-2]) / level)
    return rows


def spectral_tables():
    degree = NP - 1
    points = -np.cos(np.pi * np.arange(NP) / degree)
    for newton_step in range(60):
        rows = legendre_rows(points, degree)
        points = points - (points * rows[degree] - rows[degree - 1]) / (NP * rows[degree])
    rows = legendre_rows(points, degree)
    weights = 2.0 / (degree * NP * rows[degree] ** 2)
    spacing = points[:, None] - points[None, :] + np.eye(NP)
    matrix = rows[degree][:, None] / rows[degree][None, :] / spacing
    corner = np.concatenate([[-degree * NP / 4.0], np.zeros(NP - 2), [degree * NP / 4.0]])
    matrix = matrix * (1.0 - np.eye(NP)) + np.eye(NP) * corner[None, :]
    unit = np.eye(NP)
    along_azim = np.kron(np.eye(2 * NP), matrix)
    along_span = np.kron(np.eye(2), np.kron(matrix, unit))
    volume = np.kron(np.kron(weights, weights), weights).reshape(4, 1, LANES)
    volume = np.broadcast_to(volume, (4, ER, LANES)).reshape(16, LANES)
    sub, lane = np.arange(8)[:, None], np.arange(LANES)[None, :]
    half, side = sub // 4, lane // 64
    radial = []
    for out in range(2):
        for m in range(2):
            for p in range(2):
                for q in range(2):
                    to = 2 * (2 * out + half) + side
                    source = 2 * (2 * m + half * (1 - p) + (1 - half) * p) + side * (1 - q) + (1 - side) * q
                    radial.append(matrix[to, source])
    return np.concatenate([along_azim.T, along_span.T] + radial + [volume], axis=0)


def split(value):
    high = value.astype(BF16)
    return high, (value - high.astype(F32)).astype(BF16)


def dot(a, b):
    return jnp.dot(a, b, preferred_element_type=F32)


def dot_t(a, b):
    return lax.dot_general(a, b, (((1,), (1,)), ((), ())), preferred_element_type=F32)


def lane_of():
    return lax.broadcasted_iota(jnp.int32, (8, LANES), 1)


def sub_of():
    return lax.broadcasted_iota(jnp.int32, (8, LANES), 0)


def terms(take, tab_ref, ij2, ijl):
    ext = [3.0 * take(0, c) - 3.0 * take(0, 3 + c) + take(0, 6 + c) for c in range(3)]
    n = ext[0].shape[0]
    high, low = split(jnp.concatenate(ext, axis=0))
    s_ij = dot(jnp.concatenate([high, low], axis=1), ij2[...]) + dot(high, ijl[...])
    m0, m1, m2 = (take(1, d) for d in range(3))
    volume = jnp.broadcast_to(tab_ref[384:, :][None], (n // 16, 16, LANES)).reshape(n, LANES)
    mass = volume / (m0 * m1 * m2)
    a0, a1, a2 = ext[0] * m0, ext[1] * m1, ext[2] * m2
    out = []
    for c in range(3):
        part = slice(c * n, (c + 1) * n)
        pairs = ext[c].reshape(n // 16, 2, 8, LANES)
        seen = []
        for m in range(2):
            for v in (pairs[:, m], pltpu.roll(pairs[:, m], 4, 1)):
                seen += [v, pltpu.roll(v, 64, 2)]
        s_k = []
        for o in range(2):
            s_k.append(sum(v * tab_ref[256 + 64 * o + 8 * q : 264 + 64 * o + 8 * q, :] for q, v in enumerate(seen)))
        s_k = jnp.stack(s_k, axis=1).reshape(n, LANES)
        conv = a0 * s_ij[part, :LANES] + a1 * s_ij[part, LANES:] + a2 * s_k
        past = (3.0 / STEP_DT) * take(0, c) - (1.5 / STEP_DT) * take(0, 3 + c)
        past = past + (1.0 / (3.0 * STEP_DT)) * take(0, 6 + c)
        out.append(mass * (past - conv))
    return out


def place_tables(tab_ref, ij2, ijl):
    high, low = split(jnp.concatenate([tab_ref[:LANES, :], tab_ref[LANES : 2 * LANES, :]], axis=1))
    ij2[:LANES, :], ij2[LANES:, :], ijl[...] = high, high, low


def inner_sums(here):
    lane, sub = lane_of(), sub_of()
    j_of = lane // 8 % 8
    k_down = (lane < 64) & (sub >= 1) & (sub < 4)
    k_up = (lane >= 64) & (sub >= 4) & (sub < 7)
    gap = jnp.zeros((2, 8, LANES), F32)
    down = pltpu.roll(jnp.where(j_of == 0, here[2:], 0.0), 56, 2)
    up = pltpu.roll(jnp.where(j_of == 7, here[:-2], 0.0), LANES - 56, 2)
    here = here + jnp.concatenate([down, gap], axis=0) + jnp.concatenate([gap, up], axis=0)
    pairs = here.reshape(ES, 2, 8, LANES)
    inner, outer = pairs[:, 0], pairs[:, 1]
    from_above = pltpu.roll(pltpu.roll(inner, 64, 2), 3, 1)
    from_below = pltpu.roll(pltpu.roll(outer, 64, 2), 5, 1)
    inner = inner + jnp.where(k_down, from_below, 0.0)
    outer = outer + jnp.where(k_up, from_above, 0.0)
    return jnp.stack([inner, outer], axis=1)


def traces(vel, tab_ref, face_ref, side_ref, slot_ref, off_ref):
    last = pl.ds(15, SLOTS, stride=16)
    faces = [3.0 * vel[c, last, :] - 3.0 * vel[3 + c, last, :] + vel[6 + c, last, :] for c in range(3)]
    faces = jnp.concatenate(faces, axis=0)[:, 64:]
    table = tab_ref[...].reshape(NOFF * 64, 64)
    fh, fl = split(faces)
    th, tl = split(table)
    every = dot_t(fh, th) + dot_t(fh, tl) + dot_t(fl, th)
    side = side_ref[...]
    target = jnp.where(side >= 0, side * SLOTS + slot_ref[...], -1)
    hit_t = (lax.broadcasted_iota(jnp.int32, (2 * SLOTS, TL), 0) == target).astype(BF16)
    combo = off_ref[...] * SLOTS + face_ref[...]
    hit_c = (lax.broadcasted_iota(jnp.int32, (NOFF * SLOTS, TL), 0) == combo).astype(BF16)
    counts = dot_t(hit_t, hit_c).astype(BF16)
    left = (lane_of() < 64)[:1]
    zero = jnp.zeros((SLOTS, LANES), F32)
    stacked = []
    for pair in range(NOFF // 2):
        r0, r1, r2 = (every[c * SLOTS : (c + 1) * SLOTS, pair * LANES : (pair + 1) * LANES] for c in range(3))
        t0, t1, t2 = (pltpu.roll(v, 64, 1) for v in (r0, r1, r2))
        stacked.append(jnp.concatenate([jnp.where(left, r0, t1), jnp.where(left, r2, zero)], axis=1))
        stacked.append(jnp.concatenate([jnp.where(left, t0, r1), jnp.where(left, t2, zero)], axis=1))
    stacked = jnp.concatenate(stacked, axis=0)
    sh, sl = split(stacked)
    return dot(counts, sh) + dot(counts, sl)


def rim_kernel(
    face_hbm, side_hbm, slot_hbm, off_hbm, vel_hbm, met_hbm, mortar_hbm, tab_hbm,
    vel, met, tab_ref, rim_ref, e_ref, o_ref, own_ref, mortar, face_ref, side_ref, slot_ref, off_ref, ij2, ijl, sem,
):
    ends, middle = (pl.ds(0, ES), pl.ds((EA - 1) * ES, ES)), pl.ds(ES, (EA - 2) * ES)
    below, above = pl.ds(0, 8), pl.ds(8, 8)
    end_rows, mid_rows = (pl.ds(0, BLOCK), pl.ds((EA - 1) * BLOCK, BLOCK)), pl.ds(BLOCK, (EA - 2) * BLOCK)
    moves = [(tab_hbm, tab_ref)] + [(vel_hbm.at[:, part], vel.at[:, part]) for part in ends]
    moves += [(met_hbm.at[:, part], met.at[:, part]) for part in end_rows]
    moves += [(face_hbm, face_ref), (side_hbm, side_ref), (slot_hbm, slot_ref), (off_hbm, off_ref), (mortar_hbm, mortar)]
    moves += [(vel_hbm.at[:, middle, above], vel.at[:, middle, above])]
    moves += [(vel_hbm.at[:, middle, below], vel.at[:, middle, below]), (met_hbm.at[:, mid_rows], met.at[:, mid_rows])]
    copies = [pltpu.make_async_copy(source, target, sem.at[q]) for q, (source, target) in enumerate(moves)]
    for copy in copies:
        copy.start()
    is_odd = lax.axis_index("azim") % 2 == 1
    flat = vel.reshape(9, ROWS, LANES)
    copies[0].wait()
    place_tables(tab_ref, ij2, ijl)
    for copy in copies[1:5]:
        copy.wait()

    def take(kind, q):
        ref = (flat, met)[kind]
        return jnp.concatenate([ref[q, :BLOCK, :], ref[q, (EA - 1) * BLOCK :, :]], axis=0)

    raw = terms(take, tab_ref, ij2, ijl)
    lane = lane_of()
    faces = [[], []]
    for c in range(3):
        for end in range(2):
            column = raw[c][end * BLOCK : (end + 1) * BLOCK]
            rim_ref[c, end] = column
            here = inner_sums(column.reshape(8, 8, LANES))
            keep = lane % 8 == 7 * end
            face = jnp.zeros((8, LANES), F32)
            for m in range(8):
                face += pltpu.roll(jnp.where(keep, here[m // 2, m % 2], 0.0), (m - 7 * end) % LANES, 1)
            faces[end].append(face)
    low, high = jnp.concatenate(faces[0], axis=0), jnp.concatenate(faces[1], axis=0)
    e_ref[:24, :] = jnp.where(is_odd, low, high)
    o_ref[:24, :] = jnp.where(is_odd, high, low)
    for copy in copies[5:11]:
        copy.wait()
    trace = traces(flat, mortar, face_ref, side_ref, slot_ref, off_ref)
    own_ref[...] = trace[:SLOTS]
    packed = jnp.concatenate([trace[SLOTS:, :LANES], trace[SLOTS:, LANES:]], axis=0)
    e_ref[24:, :] = packed
    o_ref[24:, :] = packed
    for copy in copies[11:]:
        copy.wait()


def rest_kernel(vel, met, tab_ref, rim_ref, out_ref, span_ref, total, ij2, ijl):
    place_tables(tab_ref, ij2, ijl)
    for c in range(3):
        total[c, 0] = jnp.zeros((BLOCK, LANES), F32)
        total[c, EA + 1] = jnp.zeros((BLOCK, LANES), F32)
        total[c, 1] = rim_ref[c, 0]
        total[c, EA] = rim_ref[c, 1]
    span_ref[...] = jnp.zeros_like(span_ref)

    @pl.loop(0, (EA - 2) // WIDE)
    def _(q):
        first = 1 + q * WIDE
        rows = pl.ds(pl.multiple_of(first * BLOCK, BLOCK), WIDE * BLOCK)
        raw = terms(lambda kind, d: (vel, met)[kind][d, rows, :], tab_ref, ij2, ijl)
        for c, part in enumerate(raw):
            total[c, pl.ds(first + 1, WIDE)] = part.reshape(WIDE, BLOCK, LANES)

    lane = lane_of()
    i_of, j_of = lane % 8, lane // 8 % 8

    @pl.loop(0, EA, unroll=2)
    def _(a):
        for c in range(3):
            here, below, above = (total[c, a + d].reshape(8, 8, LANES) for d in (1, 0, 2))
            here = here + pltpu.roll(jnp.where((i_of == 0) & (a < EA - 1), above, 0.0), 7, 2)
            here = here + pltpu.roll(jnp.where((i_of == 7) & (a > 0), below, 0.0), LANES - 7, 2)
            here = inner_sums(here)
            out_ref[c, a] = here.reshape(BLOCK, LANES)
            for end in range(2):
                face = jnp.where(j_of == 7 * end, here[3 * end], 0.0)
                shift = lax.rem(8 * a + LANES - 56 * end, LANES)
                for t in range(2):
                    rows = pl.ds((c * 2 + t) * 8, 8)
                    span_ref[end, rows, :] += pltpu.roll(face[t], shift, 1)


def corner_kernel(e_ref, o_ref, span_ref, own_ref, se_ref, so_ref, low_ref, high_ref, sum_ref):
    is_odd = lax.axis_index("azim") % 2 == 1
    from_e, from_o = e_ref[...], o_ref[...]
    low = jnp.where(is_odd, from_e, from_o)
    high = jnp.where(is_odd, from_o, from_e)
    low_ref[...] = low[:24]
    high_ref[...] = high[:24]
    arrived = low[24:]
    sum_ref[...] = own_ref[...] + jnp.concatenate([arrived[:SLOTS], arrived[SLOTS:]], axis=1)
    half = lane_of() % 64
    ends = []
    for end in range(2):
        parts = []
        for c in range(3):
            for t in range(2):
                face = span_ref[end, pl.ds((c * 2 + t) * 8, 8), :]
                m = 6 * end + t
                seat = m + 56 * end
                face += jnp.where(half == 0, pltpu.roll(low[c * 8 : c * 8 + 8], -seat % LANES, 1), 0.0)
                face += jnp.where(half == 63, pltpu.roll(high[c * 8 : c * 8 + 8], (63 - seat) % LANES, 1), 0.0)
                parts.append(face)
        ends.append(jnp.concatenate(parts, axis=0))
    odd = lax.axis_index("span") % 2 == 1
    se_ref[...] = jnp.where(odd, ends[0], ends[1])
    so_ref[...] = jnp.where(odd, ends[1], ends[0])


def final_kernel(part_ref, low_ref, high_ref, se_ref, so_ref, out_hbm, work, span_faces, sem):
    middle = pl.ds(1, EA - 2)
    spots = ((middle, pl.ds(16, 32)), (0, pl.ds(0, BLOCK)), (EA - 1, pl.ds(0, BLOCK)), (middle, pl.ds(0, 16)), (middle, pl.ds(48, 16)))
    copies = [
        pltpu.make_async_copy((work if q else part_ref).at[:, a, r], out_hbm.at[:, a, r], sem.at[q]) for q, (a, r) in enumerate(spots)
    ]
    copies[0].start()
    span = lax.axis_index("span")
    odd = span % 2 == 1
    from_e, from_o = se_ref[...], so_ref[...]
    span_faces[0] = jnp.where(span == 0, 0.0, jnp.where(odd, from_e, from_o))
    span_faces[1] = jnp.where(span == lax.axis_size("span") - 1, 0.0, jnp.where(odd, from_o, from_e))
    lane = lane_of()
    i_of, j_of = lane % 8, lane // 8 % 8

    @pl.loop(0, 8, unroll=4)
    def _(m):
        rows = pl.ds(pl.multiple_of(8 * m, 8), 8)
        for end, ref in enumerate((low_ref, high_ref)):
            for c in range(3):
                face = pltpu.roll(ref[8 * c : 8 * c + 8, :], lax.rem(7 * end + LANES - m, LANES), 1)
                work[c, (EA - 1) * end, rows, :] = part_ref[c, (EA - 1) * end, rows, :] + jnp.where(i_of == 7 * end, face, 0.0)

    def edges(a, source):
        for end in range(2):
            for c in range(3):
                for t in range(2):
                    rows = pl.ds(48 * end + 8 * t, 8)
                    face = span_faces[end, (c * 2 + t) * 8 : (c * 2 + t) * 8 + 8, :]
                    face = pltpu.roll(face, lax.rem(56 * end + LANES - 8 * a, LANES), 1)
                    work[c, a, rows, :] = source[c, a, rows, :] + jnp.where(j_of == 7 * end, face, 0.0)

    for q, a in ((1, 0), (2, EA - 1)):
        edges(a, work)
        copies[q].start()

    @pl.loop(1, EA - 1, unroll=6)
    def _(a):
        edges(a, part_ref)

    copies[3].start()
    copies[4].start()
    for copy in copies:
        copy.wait()


def swap(value, axis, first):
    count = lax.axis_size(axis)
    pairs = []
    for low in range(first, count + first, 2):
        pairs += [(low % count, (low + 1) % count), ((low + 1) % count, low % count)]
    return lax.ppermute(value, axis, pairs)


def turned(value, by):
    count = lax.axis_size("azim")
    return lax.ppermute(value, "azim", [(i, (i + by) % count) for i in range(count)])


def local(velocity, metric, mortar_tables, angle_step, tile_face, tile_side, tile_slot, tile_offset):
    vel = velocity.reshape(9, EA * ES, ER, 4, LANES).transpose(0, 1, 3, 2, 4).reshape(9, ROWS, LANES)
    met = metric.reshape(3, EA * ES, ER, 4, LANES).transpose(0, 1, 3, 2, 4).reshape(3, ROWS, LANES)
    vmem = pl.BlockSpec(memory_space=pltpu.VMEM)
    hbm = pl.BlockSpec(memory_space=pltpu.HBM)
    v = lambda *shape: pltpu.VMEM(shape, F32)
    far = lambda x: pltpu.with_memory_space_constraint(x, pltpu.HBM)
    limit = lambda mib: pltpu.CompilerParams(vmem_limit_bytes=mib * 2**20)
    lists = [far(t.reshape(1, TL)) for t in (tile_face, tile_side, tile_slot, tile_offset)]
    bf16_tables = [pltpu.VMEM((256, 256), BF16), pltpu.VMEM((128, 256), BF16)]
    vel_v, met_v, tab_v, rim, to_e, to_o, own = pl.pallas_call(
        rim_kernel,
        out_shape=(
            v(9, EA * ES, 16, LANES), v(3, ROWS, LANES), v(400, LANES), v(3, 2, BLOCK, LANES), v(88, LANES), v(88, LANES), v(SLOTS, 2 * LANES)
        ),
        in_specs=[hbm] * 8,
        out_specs=[vmem] * 7,
        scratch_shapes=[pltpu.VMEM((NOFF, 64, 64), F32)]
        + [pltpu.VMEM((1, TL), jnp.int32)] * 4
        + bf16_tables
        + [pltpu.SemaphoreType.DMA((13,))],
        compiler_params=limit(24),
        name="rim_terms",
    )(*lists, far(vel.reshape(9, EA * ES, 16, LANES)), far(met), far(mortar_tables), far(jnp.asarray(spectral_tables(), F32)))
    from_e = swap(to_e, "azim", 0)
    from_o = swap(to_o, "azim", 1)
    part, span_faces = pl.pallas_call(
        rest_kernel,
        out_shape=(v(3, EA, BLOCK, LANES), v(2, 48, LANES)),
        in_specs=[vmem] * 4,
        out_specs=[vmem] * 2,
        scratch_shapes=[pltpu.VMEM((3, EA + 2, BLOCK, LANES), F32)] + bf16_tables,
        compiler_params=limit(24),
        cost_estimate=pl.CostEstimate(flops=10**9, bytes_accessed=8 * 2**20, transcendentals=0),
        name="rest_terms",
    )(vel_v.reshape(9, ROWS, LANES), met_v, tab_v, rim)
    to_se, to_so, low, high, summed = pl.pallas_call(
        corner_kernel,
        out_shape=(v(48, LANES), v(48, LANES), v(24, LANES), v(24, LANES), v(SLOTS, 2 * LANES)),
        in_specs=[vmem] * 4,
        out_specs=[vmem] * 5,
        compiler_params=limit(8),
        name="corners",
    )(from_e, from_o, span_faces, own)
    from_se = swap(to_se, "span", 0)
    from_so = swap(to_so, "span", 1)
    count = lax.axis_size("azim")
    trace = lax.switch(angle_step[0] % count, [lambda v, k=k: turned(v, k) for k in range(count)], summed)
    rhs = pl.pallas_call(
        final_kernel,
        out_shape=jax.ShapeDtypeStruct((3, EA, BLOCK, LANES), F32),
        in_specs=[vmem] * 5,
        out_specs=hbm,
        scratch_shapes=[
            pltpu.VMEM((3, EA, BLOCK, LANES), F32), pltpu.VMEM((2, 48, LANES), F32), pltpu.SemaphoreType.DMA((5,))
        ],
        compiler_params=limit(8),
        name="join",
    )(part, low, high, from_se, from_so)
    rhs = rhs.reshape(3, EA * ES, 4, ER, LANES).transpose(0, 1, 3, 2, 4).reshape(3, EA, ES, ER, 4 * LANES)
    stator = trace[:, :192].reshape(SLOTS, 3, 64)
    return rhs, stator


def solution(mesh):
    return jax.shard_map(
        local,
        mesh=mesh,
        in_specs=(
            P(None, None, "azim", "span", None, None),
            P(None, "azim", "span", None, None),
            P(),
            P(),
            P("azim", "span", None),
            P("azim", "span", None),
            P("azim", "span", None),
            P("azim", "span", None),
        ),
        out_specs=(P(None, "azim", "span", None, None), P(("azim", "span"), None, None)),
        check_vma=False,
    )
```

```python
import jax
import jax.numpy as jnp
import numpy as np
from jax import lax
from jax.experimental import pallas as pl
from jax.experimental.pallas import tpu as pltpu
from jax.sharding import PartitionSpec as P

NP = 8
STEP_DT = 0.05
EA, ES, ER = 8, 4, 4
BLOCK = ES * 16
ROWS = EA * BLOCK
LANES = 128
TL = 64
NOFF = 8
SLOTS = 32
WIDE = 3
F32 = jnp.float32
BF16 = jnp.bfloat16


def legendre_rows(points, degree):
    rows = [points * 0.0 + 1.0, points]
    for level in range(2, degree + 1):
        rows.append(((2 * level - 1) * points * rows[-1] - (level - 1) * rows[-2]) / level)
    return rows


def spectral_tables():
    degree = NP - 1
    points = -np.cos(np.pi * np.arange(NP) / degree)
    for newton_step in range(60):
        rows = legendre_rows(points, degree)
        points = points - (points * rows[degree] - rows[degree - 1]) / (NP * rows[degree])
    rows = legendre_rows(points, degree)
    weights = 2.0 / (degree * NP * rows[degree] ** 2)
    spacing = points[:, None] - points[None, :] + np.eye(NP)
    matrix = rows[degree][:, None] / rows[degree][None, :] / spacing
    corner = np.concatenate([[-degree * NP / 4.0], np.zeros(NP - 2), [degree * NP / 4.0]])
    matrix = matrix * (1.0 - np.eye(NP)) + np.eye(NP) * corner[None, :]
    unit = np.eye(NP)
    along_azim = np.kron(np.eye(2 * NP), matrix)
    along_span = np.kron(np.eye(2), np.kron(matrix, unit))
    volume = np.kron(np.kron(weights, weights), weights).reshape(4, 1, LANES)
    volume = np.broadcast_to(volume, (4, ER, LANES)).reshape(16, LANES)
    sub, lane = np.arange(8)[:, None], np.arange(LANES)[None, :]
    half, side = sub // 4, lane // 64
    radial = []
    for out in range(2):
        for m in range(2):
            for p in range(2):
                for q in range(2):
                    to = 2 * (2 * out + half) + side
                    source = 2 * (2 * m + half * (1 - p) + (1 - half) * p) + side * (1 - q) + (1 - side) * q
                    radial.append(matrix[to, source])
    return np.concatenate([along_azim.T, along_span.T] + radial + [volume], axis=0)


def split(value):
    high = value.astype(BF16)
    return high, (value - high.astype(F32)).astype(BF16)


def dot(a, b):
    return jnp.dot(a, b, preferred_element_type=F32)


def dot_t(a, b):
    return lax.dot_general(a, b, (((1,), (1,)), ((), ())), preferred_element_type=F32)


def lane_of():
    return lax.broadcasted_iota(jnp.int32, (8, LANES), 1)


def sub_of():
    return lax.broadcasted_iota(jnp.int32, (8, LANES), 0)


def terms(take, tab_ref, ij2, ijl):
    ext = [3.0 * take(0, c) - 3.0 * take(0, 3 + c) + take(0, 6 + c) for c in range(3)]
    n = ext[0].shape[0]
    high, low = split(jnp.concatenate(ext, axis=0))
    s_ij = dot(jnp.concatenate([high, low], axis=1), ij2[...]) + dot(high, ijl[...])
    m0, m1, m2 = (take(1, d) for d in range(3))
    volume = jnp.broadcast_to(tab_ref[384:, :][None], (n // 16, 16, LANES)).reshape(n, LANES)
    mass = volume / (m0 * m1 * m2)
    a0, a1, a2 = ext[0] * m0, ext[1] * m1, ext[2] * m2
    out = []
    for c in range(3):
        part = slice(c * n, (c + 1) * n)
        pairs = ext[c].reshape(n // 16, 2, 8, LANES)
        seen = []
        for m in range(2):
            for v in (pairs[:, m], pltpu.roll(pairs[:, m], 4, 1)):
                seen += [v, pltpu.roll(v, 64, 2)]
        s_k = []
        for o in range(2):
            s_k.append(sum(v * tab_ref[256 + 64 * o + 8 * q : 264 + 64 * o + 8 * q, :] for q, v in enumerate(seen)))
        s_k = jnp.stack(s_k, axis=1).reshape(n, LANES)
        conv = a0 * s_ij[part, :LANES] + a1 * s_ij[part, LANES:] + a2 * s_k
        past = (3.0 / STEP_DT) * take(0, c) - (1.5 / STEP_DT) * take(0, 3 + c)
        past = past + (1.0 / (3.0 * STEP_DT)) * take(0, 6 + c)
        out.append(mass * (past - conv))
    return out


def place_tables(tab_ref, ij2, ijl):
    high, low = split(jnp.concatenate([tab_ref[:LANES, :], tab_ref[LANES : 2 * LANES, :]], axis=1))
    ij2[:LANES, :], ij2[LANES:, :], ijl[...] = high, high, low


def inner_sums(here):
    lane, sub = lane_of(), sub_of()
    j_of = lane // 8 % 8
    k_down = (lane < 64) & (sub >= 1) & (sub < 4)
    k_up = (lane >= 64) & (sub >= 4) & (sub < 7)
    gap = jnp.zeros((2, 8, LANES), F32)
    down = pltpu.roll(jnp.where(j_of == 0, here[2:], 0.0), 56, 2)
    up = pltpu.roll(jnp.where(j_of == 7, here[:-2], 0.0), LANES - 56, 2)
    here = here + jnp.concatenate([down, gap], axis=0) + jnp.concatenate([gap, up], axis=0)
    pairs = here.reshape(ES, 2, 8, LANES)
    inner, outer = pairs[:, 0], pairs[:, 1]
    from_above = pltpu.roll(pltpu.roll(inner, 64, 2), 3, 1)
    from_below = pltpu.roll(pltpu.roll(outer, 64, 2), 5, 1)
    inner = inner + jnp.where(k_down, from_below, 0.0)
    outer = outer + jnp.where(k_up, from_above, 0.0)
    return jnp.stack([inner, outer], axis=1)


def traces(vel, tab_ref, face_ref, side_ref, slot_ref, off_ref):
    last = pl.ds(15, SLOTS, stride=16)
    faces = [3.0 * vel[c, last, :] - 3.0 * vel[3 + c, last, :] + vel[6 + c, last, :] for c in range(3)]
    faces = jnp.concatenate(faces, axis=0)[:, 64:]
    table = tab_ref[...].reshape(NOFF * 64, 64)
    fh, fl = split(faces)
    th, tl = split(table)
    every = dot_t(fh, th) + dot_t(fh, tl) + dot_t(fl, th)
    side = side_ref[...]
    target = jnp.where(side >= 0, side * SLOTS + slot_ref[...], -1)
    hit_t = (lax.broadcasted_iota(jnp.int32, (2 * SLOTS, TL), 0) == target).astype(BF16)
    combo = off_ref[...] * SLOTS + face_ref[...]
    hit_c = (lax.broadcasted_iota(jnp.int32, (NOFF * SLOTS, TL), 0) == combo).astype(BF16)
    counts = dot_t(hit_t, hit_c).astype(BF16)
    left = (lane_of() < 64)[:1]
    zero = jnp.zeros((SLOTS, LANES), F32)
    stacked = []
    for pair in range(NOFF // 2):
        r0, r1, r2 = (every[c * SLOTS : (c + 1) * SLOTS, pair * LANES : (pair + 1) * LANES] for c in range(3))
        t0, t1, t2 = (pltpu.roll(v, 64, 1) for v in (r0, r1, r2))
        stacked.append(jnp.concatenate([jnp.where(left, r0, t1), jnp.where(left, r2, zero)], axis=1))
        stacked.append(jnp.concatenate([jnp.where(left, t0, r1), jnp.where(left, t2, zero)], axis=1))
    stacked = jnp.concatenate(stacked, axis=0)
    sh, sl = split(stacked)
    return dot(counts, sh) + dot(counts, sl)


def rim_kernel(
    face_hbm, side_hbm, slot_hbm, off_hbm, vel_hbm, met_hbm, mortar_hbm, tab_hbm,
    vel, met, tab_ref, rim_ref, e_ref, o_ref, own_ref, mortar, face_ref, side_ref, slot_ref, off_ref, ij2, ijl, sem,
):
    ends, middle = (pl.ds(0, ES), pl.ds((EA - 1) * ES, ES)), pl.ds(ES, (EA - 2) * ES)
    below, above = pl.ds(0, 8), pl.ds(8, 8)
    end_rows, mid_rows = (pl.ds(0, BLOCK), pl.ds((EA - 1) * BLOCK, BLOCK)), pl.ds(BLOCK, (EA - 2) * BLOCK)
    moves = [(tab_hbm, tab_ref)] + [(vel_hbm.at[:, part], vel.at[:, part]) for part in ends]
    moves += [(met_hbm.at[:, part], met.at[:, part]) for part in end_rows]
    moves += [(face_hbm, face_ref), (side_hbm, side_ref), (slot_hbm, slot_ref), (off_hbm, off_ref), (mortar_hbm, mortar)]
    moves += [(vel_hbm.at[:, middle, above], vel.at[:, middle, above])]
    moves += [(vel_hbm.at[:, middle, below], vel.at[:, middle, below]), (met_hbm.at[:, mid_rows], met.at[:, mid_rows])]
    copies = [pltpu.make_async_copy(source, target, sem.at[q]) for q, (source, target) in enumerate(moves)]
    for copy in copies:
        copy.start()
    is_odd = lax.axis_index("azim") % 2 == 1
    flat = vel.reshape(9, ROWS, LANES)
    copies[0].wait()
    place_tables(tab_ref, ij2, ijl)
    for copy in copies[1:5]:
        copy.wait()

    def take(kind, q):
        ref = (flat, met)[kind]
        return jnp.concatenate([ref[q, :BLOCK, :], ref[q, (EA - 1) * BLOCK :, :]], axis=0)

    raw = terms(take, tab_ref, ij2, ijl)
    lane = lane_of()
    faces = [[], []]
    for c in range(3):
        for end in range(2):
            column = raw[c][end * BLOCK : (end + 1) * BLOCK]
            rim_ref[c, end] = column
            here = inner_sums(column.reshape(8, 8, LANES))
            keep = lane % 8 == 7 * end
            face = jnp.zeros((8, LANES), F32)
            for m in range(8):
                face += pltpu.roll(jnp.where(keep, here[m // 2, m % 2], 0.0), (m - 7 * end) % LANES, 1)
            faces[end].append(face)
    low, high = jnp.concatenate(faces[0], axis=0), jnp.concatenate(faces[1], axis=0)
    e_ref[:24, :] = jnp.where(is_odd, low, high)
    o_ref[:24, :] = jnp.where(is_odd, high, low)
    for copy in copies[5:11]:
        copy.wait()
    trace = traces(flat, mortar, face_ref, side_ref, slot_ref, off_ref)
    own_ref[...] = trace[:SLOTS]
    third = trace[SLOTS:, LANES:]
    third = third[: SLOTS // 2] + pltpu.roll(third[SLOTS // 2 :], 64, 1)
    packed = jnp.concatenate([trace[SLOTS:, :LANES], third], axis=0)
    e_ref[24:, :] = packed
    o_ref[24:, :] = packed
    for copy in copies[11:]:
        copy.wait()


def rest_kernel(vel, met, tab_ref, rim_ref, out_ref, span_ref, total, ij2, ijl):
    place_tables(tab_ref, ij2, ijl)
    for c in range(3):
        total[c, 0] = jnp.zeros((BLOCK, LANES), F32)
        total[c, EA + 1] = jnp.zeros((BLOCK, LANES), F32)
        total[c, 1] = rim_ref[c, 0]
        total[c, EA] = rim_ref[c, 1]
    span_ref[...] = jnp.zeros_like(span_ref)

    @pl.loop(0, (EA - 2) // WIDE)
    def _(q):
        first = 1 + q * WIDE
        rows = pl.ds(pl.multiple_of(first * BLOCK, BLOCK), WIDE * BLOCK)
        raw = terms(lambda kind, d: (vel, met)[kind][d, rows, :], tab_ref, ij2, ijl)
        for c, part in enumerate(raw):
            total[c, pl.ds(first + 1, WIDE)] = part.reshape(WIDE, BLOCK, LANES)

    lane = lane_of()
    i_of, j_of = lane % 8, lane // 8 % 8

    @pl.loop(0, EA, unroll=2)
    def _(a):
        for c in range(3):
            here, below, above = (total[c, a + d].reshape(8, 8, LANES) for d in (1, 0, 2))
            here = here + pltpu.roll(jnp.where((i_of == 0) & (a < EA - 1), above, 0.0), 7, 2)
            here = here + pltpu.roll(jnp.where((i_of == 7) & (a > 0), below, 0.0), LANES - 7, 2)
            here = inner_sums(here)
            out_ref[c, a] = here.reshape(BLOCK, LANES)
            for end in range(2):
                face = jnp.where(j_of == 7 * end, here[3 * end], 0.0)
                shift = lax.rem(8 * a + LANES - 56 * end, LANES)
                for t in range(2):
                    rows = pl.ds((c * 2 + t) * 8, 8)
                    span_ref[end, rows, :] += pltpu.roll(face[t], shift, 1)


def corner_kernel(e_ref, o_ref, span_ref, own_ref, se_ref, so_ref, low_ref, high_ref, sum_ref):
    is_odd = lax.axis_index("azim") % 2 == 1
    from_e, from_o = e_ref[...], o_ref[...]
    low = jnp.where(is_odd, from_e, from_o)
    high = jnp.where(is_odd, from_o, from_e)
    low_ref[...] = low[:24]
    high_ref[...] = high[:24]
    arrived = low[24:]
    third = jnp.concatenate([arrived[SLOTS:], pltpu.roll(arrived[SLOTS:], 64, 1)], axis=0)
    sum_ref[...] = own_ref[...] + jnp.concatenate([arrived[:SLOTS], third], axis=1)
    half = lane_of() % 64
    ends = []
    for end in range(2):
        parts = []
        for c in range(3):
            for t in range(2):
                face = span_ref[end, pl.ds((c * 2 + t) * 8, 8), :]
                m = 6 * end + t
                seat = m + 56 * end
                face += jnp.where(half == 0, pltpu.roll(low[c * 8 : c * 8 + 8], -seat % LANES, 1), 0.0)
                face += jnp.where(half == 63, pltpu.roll(high[c * 8 : c * 8 + 8], (63 - seat) % LANES, 1), 0.0)
                parts.append(face)
        ends.append(jnp.concatenate(parts, axis=0))
    odd = lax.axis_index("span") % 2 == 1
    se_ref[...] = jnp.where(odd, ends[0], ends[1])
    so_ref[...] = jnp.where(odd, ends[1], ends[0])


def final_kernel(part_ref, low_ref, high_ref, se_ref, so_ref, out_hbm, work, span_faces, sem):
    middle = pl.ds(1, EA - 2)
    spots = ((middle, pl.ds(16, 32)), (0, pl.ds(0, BLOCK)), (EA - 1, pl.ds(0, BLOCK)), (middle, pl.ds(0, 16)), (middle, pl.ds(48, 16)))
    copies = [
        pltpu.make_async_copy((work if q else part_ref).at[:, a, r], out_hbm.at[:, a, r], sem.at[q]) for q, (a, r) in enumerate(spots)
    ]
    copies[0].start()
    span = lax.axis_index("span")
    odd = span % 2 == 1
    from_e, from_o = se_ref[...], so_ref[...]
    span_faces[0] = jnp.where(span == 0, 0.0, jnp.where(odd, from_e, from_o))
    span_faces[1] = jnp.where(span == lax.axis_size("span") - 1, 0.0, jnp.where(odd, from_o, from_e))
    lane = lane_of()
    i_of, j_of = lane % 8, lane // 8 % 8

    @pl.loop(0, 8, unroll=4)
    def _(m):
        rows = pl.ds(pl.multiple_of(8 * m, 8), 8)
        for end, ref in enumerate((low_ref, high_ref)):
            for c in range(3):
                face = pltpu.roll(ref[8 * c : 8 * c + 8, :], lax.rem(7 * end + LANES - m, LANES), 1)
                work[c, (EA - 1) * end, rows, :] = part_ref[c, (EA - 1) * end, rows, :] + jnp.where(i_of == 7 * end, face, 0.0)

    def edges(a, source):
        for end in range(2):
            for c in range(3):
                for t in range(2):
                    rows = pl.ds(48 * end + 8 * t, 8)
                    face = span_faces[end, (c * 2 + t) * 8 : (c * 2 + t) * 8 + 8, :]
                    face = pltpu.roll(face, lax.rem(56 * end + LANES - 8 * a, LANES), 1)
                    work[c, a, rows, :] = source[c, a, rows, :] + jnp.where(j_of == 7 * end, face, 0.0)

    for q, a in ((1, 0), (2, EA - 1)):
        edges(a, work)
        copies[q].start()

    @pl.loop(1, EA - 1, unroll=6)
    def _(a):
        edges(a, part_ref)

    copies[3].start()
    copies[4].start()
    for copy in copies:
        copy.wait()


def swap(value, axis, first):
    count = lax.axis_size(axis)
    pairs = []
    for low in range(first, count + first, 2):
        pairs += [(low % count, (low + 1) % count), ((low + 1) % count, low % count)]
    return lax.ppermute(value, axis, pairs)


def turned(value, by):
    count = lax.axis_size("azim")
    return lax.ppermute(value, "azim", [(i, (i + by) % count) for i in range(count)])


def local(velocity, metric, mortar_tables, angle_step, tile_face, tile_side, tile_slot, tile_offset):
    vel = velocity.reshape(9, EA * ES, ER, 4, LANES).transpose(0, 1, 3, 2, 4).reshape(9, ROWS, LANES)
    met = metric.reshape(3, EA * ES, ER, 4, LANES).transpose(0, 1, 3, 2, 4).reshape(3, ROWS, LANES)
    vmem = pl.BlockSpec(memory_space=pltpu.VMEM)
    hbm = pl.BlockSpec(memory_space=pltpu.HBM)
    v = lambda *shape: pltpu.VMEM(shape, F32)
    far = lambda x: pltpu.with_memory_space_constraint(x, pltpu.HBM)
    limit = lambda mib: pltpu.CompilerParams(vmem_limit_bytes=mib * 2**20)
    lists = [far(t.reshape(1, TL)) for t in (tile_face, tile_side, tile_slot, tile_offset)]
    bf16_tables = [pltpu.VMEM((256, 256), BF16), pltpu.VMEM((128, 256), BF16)]
    vel_v, met_v, tab_v, rim, to_e, to_o, own = pl.pallas_call(
        rim_kernel,
        out_shape=(
            v(9, EA * ES, 16, LANES), v(3, ROWS, LANES), v(400, LANES), v(3, 2, BLOCK, LANES), v(72, LANES), v(72, LANES), v(SLOTS, 2 * LANES)
        ),
        in_specs=[hbm] * 8,
        out_specs=[vmem] * 7,
        scratch_shapes=[pltpu.VMEM((NOFF, 64, 64), F32)]
        + [pltpu.VMEM((1, TL), jnp.int32)] * 4
        + bf16_tables
        + [pltpu.SemaphoreType.DMA((13,))],
        compiler_params=limit(24),
        name="rim_terms",
    )(*lists, far(vel.reshape(9, EA * ES, 16, LANES)), far(met), far(mortar_tables), far(jnp.asarray(spectral_tables(), F32)))
    from_e = swap(to_e, "azim", 0)
    from_o = swap(to_o, "azim", 1)
    part, span_faces = pl.pallas_call(
        rest_kernel,
        out_shape=(v(3, EA, BLOCK, LANES), v(2, 48, LANES)),
        in_specs=[vmem] * 4,
        out_specs=[vmem] * 2,
        scratch_shapes=[pltpu.VMEM((3, EA + 2, BLOCK, LANES), F32)] + bf16_tables,
        compiler_params=limit(24),
        cost_estimate=pl.CostEstimate(flops=10**9, bytes_accessed=8 * 2**20, transcendentals=0),
        name="rest_terms",
    )(vel_v.reshape(9, ROWS, LANES), met_v, tab_v, rim)
    to_se, to_so, low, high, summed = pl.pallas_call(
        corner_kernel,
        out_shape=(v(48, LANES), v(48, LANES), v(24, LANES), v(24, LANES), v(SLOTS, 2 * LANES)),
        in_specs=[vmem] * 4,
        out_specs=[vmem] * 5,
        compiler_params=limit(8),
        name="corners",
    )(from_e, from_o, span_faces, own)
    from_se = swap(to_se, "span", 0)
    from_so = swap(to_so, "span", 1)
    count = lax.axis_size("azim")
    trace = lax.switch(angle_step[0] % count, [lambda v, k=k: turned(v, k) for k in range(count)], summed)
    rhs = pl.pallas_call(
        final_kernel,
        out_shape=jax.ShapeDtypeStruct((3, EA, BLOCK, LANES), F32),
        in_specs=[vmem] * 5,
        out_specs=hbm,
        scratch_shapes=[
            pltpu.VMEM((3, EA, BLOCK, LANES), F32), pltpu.VMEM((2, 48, LANES), F32), pltpu.SemaphoreType.DMA((5,))
        ],
        compiler_params=limit(8),
        name="join",
    )(part, low, high, from_se, from_so)
    rhs = rhs.reshape(3, EA * ES, 4, ER, LANES).transpose(0, 1, 3, 2, 4).reshape(3, EA, ES, ER, 4 * LANES)
    stator = trace[:, :192].reshape(SLOTS, 3, 64)
    return rhs, stator


def solution(mesh):
    return jax.shard_map(
        local,
        mesh=mesh,
        in_specs=(
            P(None, None, "azim", "span", None, None),
            P(None, "azim", "span", None, None),
            P(),
            P(),
            P("azim", "span", None),
            P("azim", "span", None),
            P("azim", "span", None),
            P("azim", "span", None),
        ),
        out_specs=(P(None, "azim", "span", None, None), P(("azim", "span"), None, None)),
        check_vma=False,
    )
```
